32 devices in a mesh: grp: 2 (over x), ctx: 16 (over z, y, core).
Axes of the slice: x: 2, y: 2, z: 4, core: 2. Of those that a mesh axis runs over, the one named last changes fastest.
Arguments:
- queries: bfloat16 [2, 4096, 1536], P(None, ('grp', 'ctx')), parts along dimension 1, may hold values from -6 to 6
- keys: bfloat16 [4096, 1536], P(('grp', 'ctx')), parts along dimension 0, may hold values from -6 to 6
- values: bfloat16 [4096, 1536], P(('grp', 'ctx')), parts along dimension 0, may hold values from -6 to 6
- lr_tok: float32 [4096, 4], P(('grp', 'ctx')), parts along dimension 0, as said below
- lr_base: float32 [4], replicated, may hold values from 0.5 to 2
- fast_init: bfloat16 [4608, 384], replicated, may hold values from -0.3125 to 0.3125
- fast_saved: bfloat16 [9216, 384], P(('grp', 'ctx')), parts along dimension 0, may hold values from -0.3125 to 0.3125
- dout: bfloat16 [2, 4096, 1536], P(None, ('grp', 'ctx')), parts along dimension 1, may hold values from -0.59765625 to 0.59765625
Outputs:
- d_queries: bfloat16 [2, 4096, 1536], P(None, ('grp', 'ctx')), parts along dimension 1
- d_keys: bfloat16 [4096, 1536], P(('grp', 'ctx')), parts along dimension 0
- d_values: bfloat16 [4096, 1536], P(('grp', 'ctx')), parts along dimension 0
- d_lr_tok: float32 [4096, 4], P(('grp', 'ctx')), parts along dimension 0
- d_lr_base: float32 [8], P('grp'), parts along dimension 0
- d_fast_init: float32 [9216, 384], P(('grp', 'ctx')), parts along dimension 0
The draws below stay inside these ranges and needn't reach their ends.
There are 2 independent parts, one for each index of `grp`. The reference program is written for one: setup_inputs(seed, part) draws one part's arguments, and reference() takes and returns one part's arrays. A program takes and returns all parts, laid end to end along the dimension named above; an argument that names none is the same for every part. Nothing has to cross between parts.
Inputs may be any that keep to these rules, and one draw needn't show every extreme that they name: `lr_tok`: positive rates.
All inputs are finite; a program needn't handle non-finite values.
Results may differ from the reference program's by a relative error of at most 0.0012.
Values may be sent and summed in bfloat16 or wider, within the bound.
A program may use at most 128 MiB of HBM per device.

```python
import math
import jax
import jax.numpy as jnp
from jax import lax

DH = 384
HEADS = 4
SPAN = 2048
WIDTH = 1536
FW_ROWS = 4608


def draw_lr_tok(key, part):
    key_spread, key_head = jax.random.split(key)
    position = jnp.arange(SPAN, dtype=jnp.float32) / SPAN
    growth = 1.0 + 2.0 * position
    spread = jax.random.uniform(key_spread, (SPAN, HEADS), minval=0.2, maxval=1.0)
    head_scale = jax.random.uniform(key_head, (1, HEADS), minval=0.5, maxval=1.5)
    factor = 0.5 / jnp.sqrt(jnp.float32(SPAN))
    return (spread * growth[:, None] * head_scale * factor).astype(jnp.float32)


def steps_of(stream_key, extent, shards, low, top_value):
    def one(dim, blocks):
        heights = jax.random.uniform(jax.random.fold_in(jax.random.fold_in(stream_key, 6), dim), (blocks,), jnp.float32, low / len(shards), top_value / len(shards))
        return jnp.repeat(jnp.exp(heights), extent[dim] // blocks).reshape((-1,) + (1,) * (len(extent) - dim - 1))

    factor_of = one(*shards[0])
    for cut in shards[1:]:
        factor_of = factor_of * one(*cut)
    return factor_of


def noise(stream_key, dims, scale, reach, cuts=(), held_as=jnp.bfloat16):
    result = scale * jax.random.normal(stream_key, dims, jnp.float32)
    if cuts:
        result = result * steps_of(stream_key, dims, cuts, -0.22, 0.18)
    return jnp.clip(result, -reach, reach).astype(held_as)


def setup_inputs(seed: int = 0, part: int = 0) -> dict:
    seeds = jax.random.split(jax.random.key(seed), 9)
    part_keys = jax.random.split(jax.random.fold_in(seeds[8], part), 9)
    return {
        "queries": noise(part_keys[0], (2, SPAN, WIDTH), 1.0, 6.0, ((1, 16),)),
        "keys": noise(part_keys[1], (SPAN, WIDTH), 1.0, 6.0, ((0, 16),)),
        "values": noise(part_keys[2], (SPAN, WIDTH), 1.0, 6.0, ((0, 16),)),
        "lr_tok": draw_lr_tok(jax.random.fold_in(jax.random.fold_in(seeds[8], part), 71), part),
        "lr_base": jnp.clip(jnp.exp(jax.random.uniform(seeds[4], (HEADS,), jnp.float32, math.log(0.5), math.log(2.0))), 0.5, 2.0),
        "fast_init": noise(seeds[5], (FW_ROWS, DH), DH ** -0.5, 0.3125),
        "fast_saved": noise(part_keys[6], (FW_ROWS, DH), DH ** -0.5, 0.3125, ((0, 16),)),
        "dout": noise(part_keys[7], (2, SPAN, WIDTH), 0.1, 0.59765625, ((1, 16),)),
    }


def fast_apply(weights, inputs):
    gate_part = jnp.einsum('thd,hde->the', inputs, weights[0], precision=lax.Precision.HIGHEST)
    up_part = jnp.einsum('thd,hde->the', inputs, weights[1], precision=lax.Precision.HIGHEST)
    hidden = jax.nn.silu(gate_part) * up_part
    return jnp.einsum('the,hef->thf', hidden, weights[2], precision=lax.Precision.HIGHEST)

def split_heads(tokens_in, head_count):
    return tokens_in.astype(jnp.float32).reshape(tokens_in.shape[0], head_count, -1)

def query_adjoint(weights, inputs, cotangent):
    outputs, pullback = jax.vjp(fast_apply, weights, inputs)
    return pullback(cotangent)

def inner_gradient(weights, key_heads, value_heads, token_rates):

    def inner_loss(params):
        return jnp.sum(token_rates[:, :, None] * fast_apply(params, key_heads) * value_heads)
    return jax.grad(inner_loss)(weights)

def reference(queries, keys, values, lr_tok, lr_base, fast_init, fast_saved, dout):
    head_count = lr_base.shape[0]
    head_size = fast_init.shape[1]
    shape_four = (3, head_count, head_size, head_size)
    fast_zero = fast_init.astype(jnp.float32).reshape(shape_four)
    fast_one = fast_saved.astype(jnp.float32).reshape(shape_four)
    grad_one, query_one = query_adjoint(fast_one, split_heads(queries[1], head_count), split_heads(dout[1], head_count))
    grad_zero, query_zero = query_adjoint(fast_zero, split_heads(queries[0], head_count), split_heads(dout[0], head_count))
    key_heads = split_heads(keys, head_count)
    value_heads = split_heads(values, head_count)
    token_rates = lr_tok * lr_base[None, :]
    outputs, pullback = jax.vjp(inner_gradient, fast_zero, key_heads, value_heads, token_rates)
    second, key_grad, value_grad, rate_grad = pullback(grad_one)
    summed = grad_one + second + grad_zero
    token_count = queries.shape[1]
    d_queries = jnp.stack([query_zero, query_one]).reshape(2, token_count, -1).astype(jnp.bfloat16)
    d_keys = key_grad.reshape(token_count, -1).astype(jnp.bfloat16)
    d_values = value_grad.reshape(token_count, -1).astype(jnp.bfloat16)
    d_lr_tok = rate_grad * lr_base[None, :]
    d_lr_base = lax.optimization_barrier(jnp.sum(rate_grad * lr_tok, axis=0))
    return (d_queries, d_keys, d_values, d_lr_tok, d_lr_base, summed.reshape(-1, head_size))
```

```python
import functools

import jax
import jax.numpy as jnp
from jax import lax
from jax.experimental import pallas as pl
from jax.experimental.pallas import tpu as pltpu
from jax.sharding import PartitionSpec as P

MESH = pl.DeviceIdType.MESH
BF = jnp.bfloat16
F32 = jnp.float32


def split(x):
    hi = x.astype(BF)
    return hi, (x - hi.astype(F32)).astype(BF)


def dg(a, b, ca, cb):
    return lax.dot_general(a, b, (((ca,), (cb,)), ((), ())), preferred_element_type=F32)


def nn(a, b):
    return dg(a, b, 1, 0)


def nt(a, b):
    return dg(a, b, 1, 1)


def tn(a, b):
    return dg(a, b, 0, 0)


def two(op, a, b):
    if isinstance(a, tuple) and isinstance(b, tuple):
        return op(a[0], b[0]) + (op(a[0], b[1]) + op(a[1], b[0]))
    if isinstance(a, tuple):
        return op(a[0], b) + op(a[1], b)
    return op(a, b[0]) + op(a, b[1])


def gate_terms(gate):
    logistic = 1.0 / (1.0 + jnp.exp(-gate))
    return logistic, gate * logistic, logistic * (1.0 + gate * (1.0 - logistic))


def query_terms(x, g, w1, w3, w2):
    gate, up, d_hidden = nn(x, w1), nn(x, w3), nt(g, w2)
    _, activated, slope = gate_terms(gate)
    return split(d_hidden * up * slope), split(d_hidden * activated), split(activated * up)


class Copy:
    def __init__(self, me, dest, src, dst, send, recv):
        self.away = dest != me
        self.remote = pltpu.make_async_remote_copy(
            src_ref=src, dst_ref=dst, send_sem=send, recv_sem=recv,
            device_id={"ctx": dest}, device_id_type=MESH)
        self.near = pltpu.make_async_copy(src, dst, recv)

    def start(self):
        @pl.when(self.away)
        def _():
            self.remote.start()

        @pl.when(jnp.logical_not(self.away))
        def _():
            self.near.start()

    def wait_send(self):
        @pl.when(self.away)
        def _():
            self.remote.wait_send()


def arrived(buf, sem):
    pltpu.make_async_copy(buf, buf, sem).wait()


def body(sz, q_ref, do_ref, k_ref, v_ref, lr_ref, base_ref, init_ref, saved_ref,
         dq_ref, dk_ref, dv_ref, rate_ref, part_ref, fast_ref,
         line, rest, lrs, w1buf, w0buf, adj, tot, sib, fbuf, stage, rows, tile,
         s_line, r_line, s_fwd, r_fwd, s_sib, r_sib, s_rest, r_rest, s_lr, r_lr,
         s_w, r_w, s_wf, r_init, s_out, r_out, s_rate, r_rate, s_tile, r_tile,
         s_half, r_half, s_fin, r_fin):
    n, heads, group, chips, tb, dh, grain, k, pieces = sz
    me = lax.axis_index("ctx")
    h = me // group
    j = lax.rem(me, group)
    chip, core = j // 2, lax.rem(j, 2)
    other = h * group + chip * 2 + (1 - core)
    own = pieces

    def cols(i):
        return pl.ds(pl.multiple_of(i * dh, 128), dh)

    barrier = pltpu.get_barrier_semaphore()
    for step in range(1, n):
        pl.semaphore_signal(barrier, inc=1, device_id={"ctx": lax.rem(me + step, n)},
                            device_id_type=MESH)
    init_copies = [pltpu.make_async_copy(
        init_ref.at[pl.ds(pl.multiple_of((m * heads + h) * dh, 16), dh)], w0buf.at[m], r_init.at[m])
        for m in range(3)]
    for c in init_copies:
        c.start()
    pl.semaphore_wait(barrier, n - 1)

    sends = []

    def go(copy):
        copy.start()
        sends.append(copy)

    for step in (2, 1, 3, 0):
        hh = lax.rem(h + step, heads)
        for t, ref in ((0, q_ref), (1, do_ref)):
            go(Copy(me, hh * group + j, ref.at[1, :, cols(hh)], line.at[j, h, t],
                    s_line.at[step, t], r_line.at[h, t]))
    for pp in range(own):
        p = me * own + pp
        block = p // k
        slot = (block // heads) * k + lax.rem(p, k)
        for c in range(chips):
            go(Copy(me, lax.rem(block, heads) * group + c * 2 + core, saved_ref.at[pp],
                    w1buf.at[slot], s_w.at[pp, c], r_w.at[slot]))

    fwd = []
    for step in (0, 1, 3, 2):
        s = lax.rem(h + step, heads)
        for t in range(2):
            arrived(line.at[j, s, t], r_line.at[s, t])
        for d in range(1, chips):
            cc = lax.rem(chip + d, chips)
            c = pltpu.make_async_remote_copy(
                src_ref=line.at[j, s], dst_ref=line.at[j, s], send_sem=s_fwd.at[d, s],
                recv_sem=r_fwd.at[chip, s], device_id={"ctx": h * group + cc * 2 + core},
                device_id_type=MESH)
            c.start()
            fwd.append(c)
        c = pltpu.make_async_remote_copy(
            src_ref=line.at[j, s], dst_ref=line.at[j, s], send_sem=s_sib.at[chip, s],
            recv_sem=r_sib.at[chip, s], device_id={"ctx": other}, device_id_type=MESH)
        c.start()
        fwd.append(c)

    for m in range(3):
        for r in range(k):
            slot = m * k + r
            owner = ((m * heads + h) * k + r) // own
            arrived(w1buf.at[slot], r_w.at[slot])
            c = pltpu.make_async_remote_copy(
                src_ref=w1buf.at[slot], dst_ref=w1buf.at[slot], send_sem=s_wf.at[slot],
                recv_sem=r_w.at[slot], device_id={"ctx": other}, device_id_type=MESH)

            @pl.when(lax.rem(owner, 2) == core)
            def _():
                c.start()

    for t, ref in ((0, k_ref), (1, v_ref), (2, q_ref), (3, do_ref)):
        for step in (2, 1, 3, 0):
            hh = lax.rem(h + step, heads)
            src = ref.at[:, cols(hh)] if t < 2 else ref.at[0, :, cols(hh)]
            go(Copy(me, hh * group + j, src, rest.at[t, h], s_rest.at[t, step], r_rest.at[t, h]))
    for step in range(heads):
        hh = lax.rem(h + step, heads)
        go(Copy(me, hh * group + j, lr_ref.at[hh], lrs.at[h], s_lr.at[step], r_lr.at[h]))

    def saved(m):
        return w1buf[m * k:(m + 1) * k][:, :grain].reshape(dh, dh)

    def send_back(t, value, out):
        stage[t] = value.astype(BF).reshape(heads, tb, dh)
        for step in (2, 1, 3, 0):
            s = lax.rem(h + step, heads)
            go(Copy(me, s * group + j, stage.at[t, s], out, s_out.at[t, step], r_out.at[t, h]))

    adj[...] = jnp.zeros_like(adj)

    def grad_chunk(jj, mine):
        x = line[jj, :, 0].reshape(heads * tb, dh)
        g = line[jj, :, 1].reshape(heads * tb, dh)
        w1, w3, w2 = saved(0), saved(1), saved(2)
        d_gate, d_up, hidden = query_terms(x, g, w1, w3, w2)
        adj[0] += two(tn, x, d_gate)
        adj[1] += two(tn, x, d_up)
        adj[2] += two(tn, hidden, g)
        if mine:
            send_back(1, two(nt, d_gate, w1) + two(nt, d_up, w3), dq_ref.at[1, :, cols(h)])

    grad_chunk(j, True)
    def chip_step(d, _):
        cc = lax.rem(chip + d, chips)
        jj = cc * 2 + core
        for s in range(heads):
            arrived(line.at[jj, s], r_fwd.at[cc, s])
            pltpu.make_async_remote_copy(
                src_ref=line.at[jj, s], dst_ref=line.at[jj, s], send_sem=s_sib.at[cc, s],
                recv_sem=r_sib.at[cc, s], device_id={"ctx": other}, device_id_type=MESH).start()
        grad_chunk(jj, False)
        return 0

    def sib_step(d, _):
        cc = lax.rem(chip + d, chips)
        jj = cc * 2 + (1 - core)
        for s in range(heads):
            arrived(line.at[jj, s], r_sib.at[cc, s])
        grad_chunk(jj, False)
        return 0

    lax.fori_loop(1, chips, chip_step, 0)
    lax.fori_loop(0, chips, sib_step, 0)

    for c in init_copies:
        c.wait()
    for t in range(4):
        for s in range(heads):
            arrived(rest.at[t, s], r_rest.at[t, s])
    for s in range(heads):
        arrived(lrs.at[s], r_lr.at[s])
    tokens = heads * tb
    w1, w3, w2 = w0buf[0], w0buf[1], w0buf[2]
    first = (j == 0).astype(F32)

    def put(m, value):
        value = value + adj[m] * first
        tot[m * k:(m + 1) * k] = value.reshape(k, grain, dh)

    x, g = rest[2].reshape(tokens, dh), rest[3].reshape(tokens, dh)
    d_gate, d_up, hidden = query_terms(x, g, w1, w3, w2)
    put(0, two(tn, x, d_gate))
    put(1, two(tn, x, d_up))
    put(2, two(tn, hidden, g))
    send_back(0, two(nt, d_gate, w1) + two(nt, d_up, w3), dq_ref.at[0, :, cols(h)])

    keys, vals = rest[0].reshape(tokens, dh), rest[1].reshape(tokens, dh)
    base = base_ref[h]
    eta = jnp.concatenate(
        [jnp.broadcast_to(lrs[s][0:1], (tb, tb)).T[:, 0:1] for s in range(heads)], axis=0) * base
    a1, a3, a2 = split(adj[0]), split(adj[1]), split(adj[2])
    gate, up = nn(keys, w1), nn(keys, w3)
    d_hidden = eta * nt(vals, w2)
    proj1, proj3 = two(nn, keys, a1), two(nn, keys, a3)
    back = eta * two(nt, vals, a2)
    logistic, activated, slope = gate_terms(gate)
    curve = logistic * (1.0 - logistic) * (2.0 + gate * (1.0 - 2.0 * logistic))
    us = up * slope
    mixed = proj1 * us + proj3 * activated
    bar_gate = split(d_hidden * (proj1 * up * curve + proj3 * slope) + back * us)
    bar_up = split(d_hidden * proj1 * slope + back * activated)

    def more(m, value):
        tot[m * k:(m + 1) * k] += value.reshape(k, grain, dh)

    more(0, two(tn, keys, bar_gate))
    more(1, two(tn, keys, bar_up))
    more(2, two(tn, split(eta * mixed), vals))

    half = 3 * k // 2
    halves = []
    for i in range(half):
        c = pltpu.make_async_remote_copy(
            src_ref=tot.at[2 * i + 1 - core], dst_ref=sib.at[i], send_sem=s_half.at[i],
            recv_sem=r_half.at[i], device_id={"ctx": other}, device_id_type=MESH)
        c.start()
        halves.append(c)

    d_scaled = two(nn, split(mixed), w2) + two(nn, split(activated * up), a2)
    send_back(3, eta * d_scaled, dv_ref.at[:, cols(h)])
    rate = jnp.sum(vals.astype(F32) * d_scaled, axis=1, keepdims=True)
    acc = jnp.zeros((8, tb), F32)
    for s in range(heads):
        row = jnp.broadcast_to(rate[s * tb:(s + 1) * tb], (tb, tb)).T[0:8]
        rows[s] = row * base
        acc = acc + row * lrs[s]
    tile[...] = acc
    for step in range(heads):
        s = lax.rem(h + step, heads)
        go(Copy(me, s * group + j, rows.at[s], rate_ref.at[h], s_rate.at[step], r_rate.at[h]))
    for step in range(n):
        go(Copy(me, lax.rem(me + step, n), tile, part_ref.at[me], s_tile.at[step], r_tile.at[me]))

    key_grad = two(nt, bar_gate, w1) + two(nt, bar_up, w3)
    key_grad = key_grad + two(nt, split(d_hidden * us), a1)
    key_grad = key_grad + two(nt, split(d_hidden * activated), a3)
    send_back(2, key_grad, dk_ref.at[:, cols(h)])

    for i in range(half):
        halves[i].wait_recv()
        slot = 2 * i + core
        sib[i] = sib[i] + tot[slot]
        p = ((slot // k) * heads + h) * k + lax.rem(slot, k)
        go(Copy(me, p // own, sib.at[i], fbuf.at[lax.rem(p, own), chip], s_fin.at[i],
                r_fin.at[lax.rem(p, own), chip]))

    for pp in range(own):
        for c in range(chips):
            arrived(fbuf.at[pp, c], r_fin.at[pp, c])
        total = fbuf[pp, 0]
        for c in range(1, chips):
            total = total + fbuf[pp, c]
        fast_ref[pp] = total

    for s in range(heads):
        arrived(dq_ref.at[0, :, cols(s)], r_out.at[0, s])
        arrived(dq_ref.at[1, :, cols(s)], r_out.at[1, s])
        arrived(dk_ref.at[:, cols(s)], r_out.at[2, s])
        arrived(dv_ref.at[:, cols(s)], r_out.at[3, s])
        arrived(rate_ref.at[s], r_rate.at[s])
    for i in range(n):
        arrived(part_ref.at[i], r_tile.at[i])
    for c in sends:
        c.wait_send()
    for c in fwd + halves:
        c.wait_send()
    for d in range(1, chips):
        cc = lax.rem(chip + d, chips)
        for s in range(heads):
            pltpu.make_async_remote_copy(
                src_ref=line.at[cc * 2 + core, s], dst_ref=line.at[cc * 2 + core, s],
                send_sem=s_sib.at[cc, s], recv_sem=r_sib.at[cc, s],
                device_id={"ctx": other}, device_id_type=MESH).wait_send()
    for m in range(3):
        for r in range(k):
            slot = m * k + r
            owner = ((m * heads + h) * k + r) // own

            @pl.when(lax.rem(owner, 2) == core)
            def _():
                pltpu.make_async_remote_copy(
                    src_ref=w1buf.at[slot], dst_ref=w1buf.at[slot], send_sem=s_wf.at[slot],
                    recv_sem=r_w.at[slot], device_id={"ctx": other},
                    device_id_type=MESH).wait_send()


def gcd(a, b):
    while b:
        a, b = b, a % b
    return a


def local(n, queries, keys, values, lr_tok, lr_base, fast_init, fast_saved, dout):
    heads, dh = lr_base.shape[0], fast_init.shape[1]
    share, tb = fast_saved.shape[0], keys.shape[0]
    grain = gcd(share, dh)
    pad = -grain % 16
    k, own = dh // grain, share // grain
    group = n // heads
    chips = group // 2
    slots = 3 * k
    saved = jnp.pad(fast_saved.reshape(own, grain, dh), ((0, 0), (0, pad), (0, 0)))
    lr_rows = jnp.broadcast_to(lr_tok.T[:, None, :], (heads, 8, tb))
    dma = pltpu.SemaphoreType.DMA
    vmem = pl.BlockSpec(memory_space=pltpu.VMEM)
    width = heads * dh
    outs = pl.pallas_call(
        functools.partial(body, (n, heads, group, chips, tb, dh, grain, k, own)),
        out_shape=(
            jax.ShapeDtypeStruct((2, tb, width), BF),
            jax.ShapeDtypeStruct((tb, width), BF),
            jax.ShapeDtypeStruct((tb, width), BF),
            jax.ShapeDtypeStruct((heads, 8, tb), F32),
            jax.ShapeDtypeStruct((n, 8, tb), F32),
            jax.ShapeDtypeStruct((own, grain, dh), F32),
        ),
        in_specs=[vmem] * 5 + [pl.BlockSpec(memory_space=pltpu.SMEM),
                               pl.BlockSpec(memory_space=pl.ANY), vmem],
        out_specs=tuple([vmem] * 6),
        scratch_shapes=[
            pltpu.VMEM((group, heads, 2, tb, dh), BF),
            pltpu.VMEM((4, heads, tb, dh), BF),
            pltpu.VMEM((heads, 8, tb), F32),
            pltpu.VMEM((slots, grain + pad, dh), BF),
            pltpu.VMEM((3, dh, dh), BF),
            pltpu.VMEM((3, dh, dh), F32),
            pltpu.VMEM((slots, grain, dh), F32),
            pltpu.VMEM((slots // 2, grain, dh), F32),
            pltpu.VMEM((own, chips, grain, dh), F32),
            pltpu.VMEM((4, heads, tb, dh), BF),
            pltpu.VMEM((heads, 8, tb), F32),
            pltpu.VMEM((8, tb), F32),
            dma((heads, 2)), dma((heads, 2)),
            dma((chips, heads)), dma((chips, heads)),
            dma((chips, heads)), dma((chips, heads)),
            dma((4, heads)), dma((4, heads)),
            dma((heads,)), dma((heads,)),
            dma((own, chips)), dma((slots,)), dma((slots,)),
            dma((3,)),
            dma((4, heads)), dma((4, heads)),
            dma((heads,)), dma((heads,)),
            dma((n,)), dma((n,)),
            dma((slots // 2,)), dma((slots // 2,)),
            dma((slots // 2,)), dma((own, chips)),
        ],
        compiler_params=pltpu.CompilerParams(
            collective_id=0, has_side_effects=True, vmem_limit_bytes=52 * 2**20),
    )(queries, dout, keys, values, lr_rows, lr_base, fast_init, saved)
    d_queries, d_keys, d_values, rate, part, fast = outs
    d_lr_tok = rate[:, 0, :].T
    base_grad = jnp.sum(part[:, 0, :].reshape(heads, -1), axis=1)
    return (d_queries, d_keys, d_values, d_lr_tok, base_grad, fast.reshape(share, dh))


def solution(mesh):
    both = ("grp", "ctx")
    rows = P(both, None)
    spans = P(None, both, None)
    in_specs = (spans, rows, rows, rows, P(), P(), rows, spans)
    out_specs = (spans, rows, rows, rows, P("grp"), rows)
    return jax.shard_map(
        functools.partial(local, mesh.shape["ctx"]), mesh=mesh, in_specs=in_specs,
        out_specs=out_specs, check_vma=False)
```

```python
import functools

import jax
import jax.numpy as jnp
from jax import lax
from jax.experimental import pallas as pl
from jax.experimental.pallas import tpu as pltpu
from jax.sharding import PartitionSpec as P

MESH = pl.DeviceIdType.MESH
BF = jnp.bfloat16
F32 = jnp.float32


def split(x):
    hi = x.astype(BF)
    return hi, (x - hi.astype(F32)).astype(BF)


def dg(a, b, ca, cb):
    return lax.dot_general(a, b, (((ca,), (cb,)), ((), ())), preferred_element_type=F32)


def nn(a, b):
    return dg(a, b, 1, 0)


def nt(a, b):
    return dg(a, b, 1, 1)


def tn(a, b):
    return dg(a, b, 0, 0)


def two(op, a, b):
    if isinstance(a, tuple) and isinstance(b, tuple):
        return op(a[0], b[0]) + (op(a[0], b[1]) + op(a[1], b[0]))
    if isinstance(a, tuple):
        return op(a[0], b) + op(a[1], b)
    return op(a, b[0]) + op(a, b[1])


def gate_terms(gate):
    logistic = 1.0 / (1.0 + jnp.exp(-gate))
    return logistic, gate * logistic, logistic * (1.0 + gate * (1.0 - logistic))


def query_terms(x, g, w1, w3, w2):
    gate, up, d_hidden = nn(x, w1), nn(x, w3), nt(g, w2)
    _, activated, slope = gate_terms(gate)
    return split(d_hidden * up * slope), split(d_hidden * activated), split(activated * up)


class Copy:
    def __init__(self, me, dest, src, dst, send, recv):
        self.away = dest != me
        self.remote = pltpu.make_async_remote_copy(
            src_ref=src, dst_ref=dst, send_sem=send, recv_sem=recv,
            device_id={"ctx": dest}, device_id_type=MESH)
        self.near = pltpu.make_async_copy(src, dst, recv)

    def start(self):
        @pl.when(self.away)
        def _():
            self.remote.start()

        @pl.when(jnp.logical_not(self.away))
        def _():
            self.near.start()

    def wait_send(self):
        @pl.when(self.away)
        def _():
            self.remote.wait_send()


def arrived(buf, sem):
    pltpu.make_async_copy(buf, buf, sem).wait()


def body(sz, q_ref, do_ref, k_ref, v_ref, lr_ref, base_ref, init_ref, saved_ref,
         dq_ref, dk_ref, dv_ref, rate_ref, part_ref, fast_ref,
         line, rest, lrs, w1buf, w0buf, adj, tot, sib, ybuf, stage, rows, back_rows, tile,
         s_line, r_line, s_fwd, r_fwd, s_sib, r_sib, s_rest, r_rest, s_lr, r_lr,
         s_w, r_w, s_wc, s_wf, r_init, s_out, r_out, s_rate, r_rate, s_tile, r_tile,
         s_half, r_half, s_y, r_y, s_fin, r_fin):
    n, heads, group, chips, tb, dh, grain, k, pieces = sz
    me = lax.axis_index("ctx")
    h = me // group
    j = lax.rem(me, group)
    chip, core = j // 2, lax.rem(j, 2)
    other = h * group + chip * 2 + (1 - core)
    own = pieces

    def cols(i):
        return pl.ds(pl.multiple_of(i * dh, 128), dh)

    barrier = pltpu.get_barrier_semaphore()
    for step in range(1, n):
        pl.semaphore_signal(barrier, inc=1, device_id={"ctx": lax.rem(me + step, n)},
                            device_id_type=MESH)
    init_copies = [pltpu.make_async_copy(
        init_ref.at[pl.ds(pl.multiple_of((m * heads + h) * dh, 16), dh)], w0buf.at[m], r_init.at[m])
        for m in range(3)]
    for c in init_copies:
        c.start()
    pl.semaphore_wait(barrier, n - 1)

    sends = []

    def go(copy):
        copy.start()
        sends.append(copy)

    for pp in range(own):
        p = me * own + pp
        block = p // k
        slot = (block // heads) * k + lax.rem(p, k)
        go(Copy(me, lax.rem(block, heads) * group + j, saved_ref.at[pp],
                w1buf.at[slot], s_w.at[pp], r_w.at[slot]))
    for step in (2, 1, 3, 0):
        hh = lax.rem(h + step, heads)
        for t, ref in ((0, q_ref), (1, do_ref)):
            go(Copy(me, hh * group + j, ref.at[1, :, cols(hh)], line.at[j, h, t],
                    s_line.at[step, t], r_line.at[h, t]))
    for s in range(heads):
        rows[s] = jnp.broadcast_to(lr_ref[s:s + 1, :], (8, tb))

    def w_copy(slot, dest, sem):
        return pltpu.make_async_remote_copy(
            src_ref=w1buf.at[slot], dst_ref=w1buf.at[slot], send_sem=sem, recv_sem=r_w.at[slot],
            device_id={"ctx": dest}, device_id_type=MESH)

    def w_each(fn):
        for slot in range(3 * k):
            owner = (((slot // k) * heads + h) * k + slot % k) // own
            fn(slot, lax.rem(owner, group))

    def w_line(slot, oj):
        @pl.when(oj == j)
        def _():
            arrived(w1buf.at[slot], r_w.at[slot])
            for d in range(1, chips):
                w_copy(slot, h * group + lax.rem(chip + d, chips) * 2 + core, s_wc.at[slot, d]).start()
            w_copy(slot, other, s_wf.at[slot]).start()

    def w_chip(slot, oj):
        @pl.when(jnp.logical_and(oj != j, lax.rem(oj, 2) == core))
        def _():
            arrived(w1buf.at[slot], r_w.at[slot])
            w_copy(slot, other, s_wf.at[slot]).start()

    def w_last(slot, oj):
        @pl.when(lax.rem(oj, 2) != core)
        def _():
            arrived(w1buf.at[slot], r_w.at[slot])

    def w_sent(slot, oj):
        @pl.when(oj == j)
        def _():
            for d in range(1, chips):
                w_copy(slot, h * group + lax.rem(chip + d, chips) * 2 + core, s_wc.at[slot, d]).wait_send()

        @pl.when(lax.rem(oj, 2) == core)
        def _():
            w_copy(slot, other, s_wf.at[slot]).wait_send()

    fwd = []
    for step in (0, 1, 3, 2):
        if step == 1:
            w_each(w_line)
        s = lax.rem(h + step, heads)
        for t in range(2):
            arrived(line.at[j, s, t], r_line.at[s, t])
        for d in range(1, chips):
            cc = lax.rem(chip + d, chips)
            c = pltpu.make_async_remote_copy(
                src_ref=line.at[j, s], dst_ref=line.at[j, s], send_sem=s_fwd.at[d, s],
                recv_sem=r_fwd.at[chip, s], device_id={"ctx": h * group + cc * 2 + core},
                device_id_type=MESH)
            c.start()
            fwd.append(c)
        c = pltpu.make_async_remote_copy(
            src_ref=line.at[j, s], dst_ref=line.at[j, s], send_sem=s_sib.at[chip, s],
            recv_sem=r_sib.at[chip, s], device_id={"ctx": other}, device_id_type=MESH)
        c.start()
        fwd.append(c)

    w_each(w_chip)

    for step in range(heads):
        hh = lax.rem(h + step, heads)
        go(Copy(me, hh * group + j, rows.at[hh], lrs.at[h], s_lr.at[step], r_lr.at[h]))
    for t, ref in ((2, q_ref), (3, do_ref), (0, k_ref), (1, v_ref)):
        for step in (2, 1, 3, 0):
            hh = lax.rem(h + step, heads)
            src = ref.at[:, cols(hh)] if t < 2 else ref.at[0, :, cols(hh)]
            go(Copy(me, hh * group + j, src, rest.at[t, h], s_rest.at[t, step], r_rest.at[t, h]))

    w_each(w_last)

    def saved(m):
        return w1buf[m * k:(m + 1) * k][:, :grain].reshape(dh, dh)

    def keep(t, value):
        stage[t] = value.astype(BF).reshape(heads, tb, dh)

    def send_back(t, out):
        for step in (2, 1, 3, 0):
            s = lax.rem(h + step, heads)
            go(Copy(me, s * group + j, stage.at[t, s], out, s_out.at[t, step], r_out.at[t, h]))

    adj[...] = jnp.zeros_like(adj)

    def grad_chunk(jj, mine):
        x = line[jj, :, 0].reshape(heads * tb, dh)
        g = line[jj, :, 1].reshape(heads * tb, dh)
        w1, w3, w2 = saved(0), saved(1), saved(2)
        d_gate, d_up, hidden = query_terms(x, g, w1, w3, w2)
        adj[0] += two(tn, x, d_gate)
        adj[1] += two(tn, x, d_up)
        adj[2] += two(tn, hidden, g)
        if mine:
            keep(1, two(nt, d_gate, w1) + two(nt, d_up, w3))

    grad_chunk(j, True)
    def chip_step(d, _):
        cc = lax.rem(chip + d, chips)
        jj = cc * 2 + core
        for s in range(heads):
            arrived(line.at[jj, s], r_fwd.at[cc, s])
            pltpu.make_async_remote_copy(
                src_ref=line.at[jj, s], dst_ref=line.at[jj, s], send_sem=s_sib.at[cc, s],
                recv_sem=r_sib.at[cc, s], device_id={"ctx": other}, device_id_type=MESH).start()
        grad_chunk(jj, False)
        return 0

    def sib_step(d, _):
        cc = lax.rem(chip + d, chips)
        jj = cc * 2 + (1 - core)
        for s in range(heads):
            arrived(line.at[jj, s], r_sib.at[cc, s])
        grad_chunk(jj, False)
        return 0

    lax.fori_loop(1, chips, chip_step, 0)
    lax.fori_loop(0, chips, sib_step, 0)

    for c in init_copies:
        c.wait()
    def rest_in(t):
        for s in range(heads):
            arrived(rest.at[t, s], r_rest.at[t, s])

    rest_in(2)
    rest_in(3)
    tokens = heads * tb
    w1, w3, w2 = w0buf[0], w0buf[1], w0buf[2]
    first = (j == 0).astype(F32)

    def put(m, value):
        value = value + adj[m] * first
        tot[m * k:(m + 1) * k] = value.reshape(k, grain, dh)

    x, g = rest[2].reshape(tokens, dh), rest[3].reshape(tokens, dh)
    d_gate, d_up, hidden = query_terms(x, g, w1, w3, w2)
    put(0, two(tn, x, d_gate))
    put(1, two(tn, x, d_up))
    put(2, two(tn, hidden, g))
    keep(0, two(nt, d_gate, w1) + two(nt, d_up, w3))
    rest_in(0)
    rest_in(1)
    send_back(1, dq_ref.at[1, :, cols(h)])
    send_back(0, dq_ref.at[0, :, cols(h)])
    for s in range(heads):
        arrived(lrs.at[s], r_lr.at[s])

    keys, vals = rest[0].reshape(tokens, dh), rest[1].reshape(tokens, dh)
    base = base_ref[h]
    eta = jnp.concatenate(
        [jnp.broadcast_to(lrs[s][0:1], (tb, tb)).T[:, 0:1] for s in range(heads)], axis=0) * base
    a1, a3, a2 = split(adj[0]), split(adj[1]), split(adj[2])
    gate, up = nn(keys, w1), nn(keys, w3)
    d_hidden = eta * nt(vals, w2)
    proj1, proj3 = two(nn, keys, a1), two(nn, keys, a3)
    back = eta * two(nt, vals, a2)
    logistic, activated, slope = gate_terms(gate)
    curve = logistic * (1.0 - logistic) * (2.0 + gate * (1.0 - 2.0 * logistic))
    us = up * slope
    mixed = proj1 * us + proj3 * activated
    bar_gate = split(d_hidden * (proj1 * up * curve + proj3 * slope) + back * us)
    bar_up = split(d_hidden * proj1 * slope + back * activated)

    def more(m, value):
        tot[m * k:(m + 1) * k] += value.reshape(k, grain, dh)

    more(0, two(tn, keys, bar_gate))
    more(1, two(tn, keys, bar_up))
    more(2, two(tn, split(eta * mixed), vals))

    half = 3 * k // 2
    halves = []
    for i in range(half):
        c = pltpu.make_async_remote_copy(
            src_ref=tot.at[2 * i + 1 - core], dst_ref=sib.at[i], send_sem=s_half.at[i],
            recv_sem=r_half.at[i], device_id={"ctx": other}, device_id_type=MESH)
        c.start()
        halves.append(c)

    d_scaled = two(nn, split(mixed), w2) + two(nn, split(activated * up), a2)
    keep(3, eta * d_scaled)
    send_back(3, dv_ref.at[:, cols(h)])
    rate = jnp.sum(vals.astype(F32) * d_scaled, axis=1, keepdims=True)
    acc = jnp.zeros((8, tb), F32)
    for s in range(heads):
        row = jnp.broadcast_to(rate[s * tb:(s + 1) * tb], (tb, tb)).T[0:8]
        back_rows[s] = row * base
        acc = acc + row * lrs[s]
    tile[...] = acc
    for step in range(heads):
        s = lax.rem(h + step, heads)
        go(Copy(me, s * group + j, back_rows.at[s], rate_ref.at[h], s_rate.at[step], r_rate.at[h]))
    for step in range(n):
        go(Copy(me, lax.rem(me + step, n), tile, part_ref.at[me], s_tile.at[step], r_tile.at[me]))

    for i in range(half):
        halves[i].wait_recv()
        sib[i] = sib[i] + tot[2 * i + core]
    per = half // chips
    for d in range(1, chips):
        cc = lax.rem(chip + d, chips)
        for i in range(per):
            c = pltpu.make_async_remote_copy(
                src_ref=sib.at[cc * per + i], dst_ref=ybuf.at[i, chips - d], send_sem=s_y.at[i, d],
                recv_sem=r_y.at[i, chips - d], device_id={"ctx": h * group + cc * 2 + core},
                device_id_type=MESH)
            c.start()
            fwd.append(c)

    key_grad = two(nt, bar_gate, w1) + two(nt, bar_up, w3)
    key_grad = key_grad + two(nt, split(d_hidden * us), a1)
    key_grad = key_grad + two(nt, split(d_hidden * activated), a3)
    keep(2, key_grad)
    send_back(2, dk_ref.at[:, cols(h)])

    for i in range(per):
        for d in range(1, chips):
            arrived(ybuf.at[i, d], r_y.at[i, d])
        x = chip * per + i
        total = sib[x]
        for d in range(1, chips):
            total = total + ybuf[i, d]
        ybuf[i, 0] = total
        slot = 2 * x + core
        p = ((slot // k) * heads + h) * k + lax.rem(slot, k)
        go(Copy(me, p // own, ybuf.at[i, 0], fast_ref.at[lax.rem(p, own)], s_fin.at[i],
                r_fin.at[lax.rem(p, own)]))

    for pp in range(own):
        arrived(fast_ref.at[pp], r_fin.at[pp])
    for s in range(heads):
        arrived(dq_ref.at[0, :, cols(s)], r_out.at[0, s])
        arrived(dq_ref.at[1, :, cols(s)], r_out.at[1, s])
        arrived(dk_ref.at[:, cols(s)], r_out.at[2, s])
        arrived(dv_ref.at[:, cols(s)], r_out.at[3, s])
        arrived(rate_ref.at[s], r_rate.at[s])
    for i in range(n):
        arrived(part_ref.at[i], r_tile.at[i])
    for c in sends:
        c.wait_send()
    for c in fwd + halves:
        c.wait_send()
    for d in range(1, chips):
        cc = lax.rem(chip + d, chips)
        for s in range(heads):
            pltpu.make_async_remote_copy(
                src_ref=line.at[cc * 2 + core, s], dst_ref=line.at[cc * 2 + core, s],
                send_sem=s_sib.at[cc, s], recv_sem=r_sib.at[cc, s],
                device_id={"ctx": other}, device_id_type=MESH).wait_send()
    w_each(w_sent)


def write_out(group, dq, dk, dv, rate, part, fast, o_dq, o_dk, o_dv, o_rate, o_base, o_fast, sem):
    own, grain, _ = fast.shape
    pairs = [(dq.at[0], o_dq.at[0]), (dq.at[1], o_dq.at[1]), (dk, o_dk), (dv, o_dv)]
    pairs += [(fast.at[i], o_fast.at[pl.ds(i * grain, grain)]) for i in range(own)]
    copies = [pltpu.make_async_copy(a, b, sem.at[i]) for i, (a, b) in enumerate(pairs)]
    for c in copies:
        c.start()
    heads = rate.shape[0]
    for s in range(heads):
        o_rate[s:s + 1, :] = rate[s, 0:1, :]
    for s in range(heads):
        o_base[s] = jnp.sum(jnp.sum(part[s * group:(s + 1) * group], axis=0)[0:1])
    for c in copies:
        c.wait()


def gcd(a, b):
    while b:
        a, b = b, a % b
    return a


def local(n, queries, keys, values, lr_tok, lr_base, fast_init, fast_saved, dout):
    heads, dh = lr_base.shape[0], fast_init.shape[1]
    share, tb = fast_saved.shape[0], keys.shape[0]
    grain = gcd(share, dh)
    pad = -grain % 16
    k, own = dh // grain, share // grain
    group = n // heads
    chips = group // 2
    slots = 3 * k
    saved = jnp.pad(fast_saved.reshape(own, grain, dh), ((0, 0), (0, pad), (0, 0)))
    dma = pltpu.SemaphoreType.DMA
    vmem = pl.BlockSpec(memory_space=pltpu.VMEM)
    anyw = pl.BlockSpec(memory_space=pl.ANY)
    width = heads * dh
    outs = pl.pallas_call(
        functools.partial(body, (n, heads, group, chips, tb, dh, grain, k, own)),
        out_shape=(
            jax.ShapeDtypeStruct((2, tb, width), BF),
            jax.ShapeDtypeStruct((tb, width), BF),
            jax.ShapeDtypeStruct((tb, width), BF),
            jax.ShapeDtypeStruct((heads, 8, tb), F32),
            jax.ShapeDtypeStruct((n, 8, tb), F32),
            jax.ShapeDtypeStruct((own, grain, dh), F32),
        ),
        in_specs=[anyw] * 4 + [vmem, pl.BlockSpec(memory_space=pltpu.SMEM), anyw, anyw],
        out_specs=(anyw, anyw, anyw, vmem, vmem, anyw),
        scratch_shapes=[
            pltpu.VMEM((group, heads, 2, tb, dh), BF),
            pltpu.VMEM((4, heads, tb, dh), BF),
            pltpu.VMEM((heads, 8, tb), F32),
            pltpu.VMEM((slots, grain + pad, dh), BF),
            pltpu.VMEM((3, dh, dh), BF),
            pltpu.VMEM((3, dh, dh), F32),
            pltpu.VMEM((slots, grain, dh), F32),
            pltpu.VMEM((slots // 2, grain, dh), F32),
            pltpu.VMEM((slots // 2 // chips, chips, grain, dh), F32),
            pltpu.VMEM((4, heads, tb, dh), BF),
            pltpu.VMEM((heads, 8, tb), F32),
            pltpu.VMEM((heads, 8, tb), F32),
            pltpu.VMEM((8, tb), F32),
            dma((heads, 2)), dma((heads, 2)),
            dma((chips, heads)), dma((chips, heads)),
            dma((chips, heads)), dma((chips, heads)),
            dma((4, heads)), dma((4, heads)),
            dma((heads,)), dma((heads,)),
            dma((own,)), dma((slots,)), dma((slots, chips)), dma((slots,)),
            dma((3,)),
            dma((4, heads)), dma((4, heads)),
            dma((heads,)), dma((heads,)),
            dma((n,)), dma((n,)),
            dma((slots // 2,)), dma((slots // 2,)),
            dma((slots // 2 // chips, chips)), dma((slots // 2 // chips, chips)),
            dma((slots // 2 // chips,)), dma((own,)),
        ],
        compiler_params=pltpu.CompilerParams(
            collective_id=0, has_side_effects=True, vmem_limit_bytes=60 * 2**20),
    )(queries, dout, keys, values, lr_tok.T, lr_base, fast_init, saved)
    d_queries, d_keys, d_values, rate, base, fast = pl.pallas_call(
        functools.partial(write_out, group),
        out_shape=(
            jax.ShapeDtypeStruct((2, tb, width), BF),
            jax.ShapeDtypeStruct((tb, width), BF),
            jax.ShapeDtypeStruct((tb, width), BF),
            jax.ShapeDtypeStruct((heads, tb), F32),
            jax.ShapeDtypeStruct((heads,), F32),
            jax.ShapeDtypeStruct((share, dh), F32),
        ),
        in_specs=[anyw] * 3 + [vmem, vmem, anyw],
        out_specs=(anyw, anyw, anyw, vmem, pl.BlockSpec(memory_space=pltpu.SMEM), anyw),
        scratch_shapes=[dma((4 + own,))],
        compiler_params=pltpu.CompilerParams(vmem_limit_bytes=60 * 2**20),
    )(*outs)
    return d_queries, d_keys, d_values, rate.T, base, fast


def solution(mesh):
    both = ("grp", "ctx")
    rows = P(both, None)
    spans = P(None, both, None)
    in_specs = (spans, rows, rows, rows, P(), P(), rows, spans)
    out_specs = (spans, rows, rows, rows, P("grp"), rows)
    return jax.shard_map(
        functools.partial(local, mesh.shape["ctx"]), mesh=mesh, in_specs=in_specs,
        out_specs=out_specs, check_vma=False)
```

```python
import functools

import jax
import jax.numpy as jnp
from jax import lax
from jax.experimental import pallas as pl
from jax.experimental.pallas import tpu as pltpu
from jax.sharding import PartitionSpec as P

MESH = pl.DeviceIdType.MESH
BF = jnp.bfloat16
F32 = jnp.float32


def split(x):
    hi = x.astype(BF)
    return hi, (x - hi.astype(F32)).astype(BF)


def dg(a, b, ca, cb):
    return lax.dot_general(a, b, (((ca,), (cb,)), ((), ())), preferred_element_type=F32)


def nn(a, b):
    return dg(a, b, 1, 0)


def nt(a, b):
    return dg(a, b, 1, 1)


def tn(a, b):
    return dg(a, b, 0, 0)


def two(op, a, b):
    if isinstance(a, tuple) and isinstance(b, tuple):
        return op(a[0], b[0]) + (op(a[0], b[1]) + op(a[1], b[0]))
    if isinstance(a, tuple):
        return op(a[0], b) + op(a[1], b)
    return op(a, b[0]) + op(a, b[1])


def gate_terms(gate):
    logistic = 1.0 / (1.0 + jnp.exp(-gate))
    return logistic, gate * logistic, logistic * (1.0 + gate * (1.0 - logistic))


def query_terms(x, g, w1, w3, w2):
    gate, up, d_hidden = nn(x, w1), nn(x, w3), nt(g, w2)
    _, activated, slope = gate_terms(gate)
    return split(d_hidden * up * slope), split(d_hidden * activated), split(activated * up)


class Copy:
    def __init__(self, me, dest, src, dst, send, recv):
        self.away = dest != me
        self.remote = pltpu.make_async_remote_copy(
            src_ref=src, dst_ref=dst, send_sem=send, recv_sem=recv,
            device_id={"ctx": dest}, device_id_type=MESH)
        self.near = pltpu.make_async_copy(src, dst, recv)

    def start(self):
        @pl.when(self.away)
        def _():
            self.remote.start()

        @pl.when(jnp.logical_not(self.away))
        def _():
            self.near.start()

    def wait_send(self):
        @pl.when(self.away)
        def _():
            self.remote.wait_send()


def arrived(buf, sem):
    pltpu.make_async_copy(buf, buf, sem).wait()


def body(sz, q_ref, do_ref, k_ref, v_ref, lr_ref, base_ref, init_ref, saved_ref,
         dq_ref, dk_ref, dv_ref, rate_ref, part_ref, fast_ref,
         line, rest, lrs, w1buf, w0buf, adj, tot, sib, fbuf, stage, rows, tile,
         s_line, r_line, s_fwd, r_fwd, s_sib, r_sib, s_rest, r_rest, s_lr, r_lr,
         s_w, r_w, s_wf, r_init, s_out, r_out, s_rate, r_rate, s_tile, r_tile,
         s_half, r_half, s_fin, r_fin):
    n, heads, group, chips, tb, dh, grain, k, pieces = sz
    me = lax.axis_index("ctx")
    h = me // group
    j = lax.rem(me, group)
    chip, core = j // 2, lax.rem(j, 2)
    other = h * group + chip * 2 + (1 - core)
    own = pieces

    def cols(i):
        return pl.ds(pl.multiple_of(i * dh, 128), dh)

    barrier = pltpu.get_barrier_semaphore()
    for step in range(1, n):
        pl.semaphore_signal(barrier, inc=1, device_id={"ctx": lax.rem(me + step, n)},
                            device_id_type=MESH)
    init_copies = [pltpu.make_async_copy(
        init_ref.at[pl.ds(pl.multiple_of((m * heads + h) * dh, 16), dh)], w0buf.at[m], r_init.at[m])
        for m in range(3)]
    for c in init_copies:
        c.start()
    pl.semaphore_wait(barrier, n - 1)

    sends = []

    def go(copy):
        copy.start()
        sends.append(copy)

    for step in (2, 1, 3, 0):
        hh = lax.rem(h + step, heads)
        for t, ref in ((0, q_ref), (1, do_ref)):
            go(Copy(me, hh * group + j, ref.at[1, :, cols(hh)], line.at[j, h, t],
                    s_line.at[step, t], r_line.at[h, t]))
    for pp in range(own):
        p = me * own + pp
        block = p // k
        slot = (block // heads) * k + lax.rem(p, k)
        for c in range(chips):
            go(Copy(me, lax.rem(block, heads) * group + c * 2 + core, saved_ref.at[pp],
                    w1buf.at[slot], s_w.at[pp, c], r_w.at[slot]))

    fwd = []
    for step in (0, 1, 3, 2):
        s = lax.rem(h + step, heads)
        for t in range(2):
            arrived(line.at[j, s, t], r_line.at[s, t])
        for d in range(1, chips):
            cc = lax.rem(chip + d, chips)
            c = pltpu.make_async_remote_copy(
                src_ref=line.at[j, s], dst_ref=line.at[j, s], send_sem=s_fwd.at[d, s],
                recv_sem=r_fwd.at[chip, s], device_id={"ctx": h * group + cc * 2 + core},
                device_id_type=MESH)
            c.start()
            fwd.append(c)
        c = pltpu.make_async_remote_copy(
            src_ref=line.at[j, s], dst_ref=line.at[j, s], send_sem=s_sib.at[chip, s],
            recv_sem=r_sib.at[chip, s], device_id={"ctx": other}, device_id_type=MESH)
        c.start()
        fwd.append(c)

    for m in range(3):
        for r in range(k):
            slot = m * k + r
            owner = ((m * heads + h) * k + r) // own
            arrived(w1buf.at[slot], r_w.at[slot])
            c = pltpu.make_async_remote_copy(
                src_ref=w1buf.at[slot], dst_ref=w1buf.at[slot], send_sem=s_wf.at[slot],
                recv_sem=r_w.at[slot], device_id={"ctx": other}, device_id_type=MESH)

            @pl.when(lax.rem(owner, 2) == core)
            def _():
                c.start()

    for t, ref in ((0, k_ref), (1, v_ref), (2, q_ref), (3, do_ref)):
        for step in (2, 1, 3, 0):
            hh = lax.rem(h + step, heads)
            src = ref.at[:, cols(hh)] if t < 2 else ref.at[0, :, cols(hh)]
            go(Copy(me, hh * group + j, src, rest.at[t, h], s_rest.at[t, step], r_rest.at[t, h]))
    for step in range(heads):
        hh = lax.rem(h + step, heads)
        go(Copy(me, hh * group + j, lr_ref.at[hh], lrs.at[h], s_lr.at[step], r_lr.at[h]))

    def saved(m):
        return w1buf[m * k:(m + 1) * k][:, :grain].reshape(dh, dh)

    def send_back(t, value, out):
        stage[t] = value.astype(BF).reshape(heads, tb, dh)
        for step in (2, 1, 3, 0):
            s = lax.rem(h + step, heads)
            go(Copy(me, s * group + j, stage.at[t, s], out, s_out.at[t, step], r_out.at[t, h]))

    adj[...] = jnp.zeros_like(adj)

    def grad_chunk(jj, mine):
        x = line[jj, :, 0].reshape(heads * tb, dh)
        g = line[jj, :, 1].reshape(heads * tb, dh)
        w1, w3, w2 = saved(0), saved(1), saved(2)
        d_gate, d_up, hidden = query_terms(x, g, w1, w3, w2)
        adj[0] += two(tn, x, d_gate)
        adj[1] += two(tn, x, d_up)
        adj[2] += two(tn, hidden, g)
        if mine:
            send_back(1, two(nt, d_gate, w1) + two(nt, d_up, w3), dq_ref.at[1, :, cols(h)])

    grad_chunk(j, True)
    def chip_step(d, _):
        cc = lax.rem(chip + d, chips)
        jj = cc * 2 + core
        for s in range(heads):
            arrived(line.at[jj, s], r_fwd.at[cc, s])
            pltpu.make_async_remote_copy(
                src_ref=line.at[jj, s], dst_ref=line.at[jj, s], send_sem=s_sib.at[cc, s],
                recv_sem=r_sib.at[cc, s], device_id={"ctx": other}, device_id_type=MESH).start()
        grad_chunk(jj, False)
        return 0

    def sib_step(d, _):
        cc = lax.rem(chip + d, chips)
        jj = cc * 2 + (1 - core)
        for s in range(heads):
            arrived(line.at[jj, s], r_sib.at[cc, s])
        grad_chunk(jj, False)
        return 0

    lax.fori_loop(1, chips, chip_step, 0)
    lax.fori_loop(0, chips, sib_step, 0)

    for c in init_copies:
        c.wait()
    for t in range(4):
        for s in range(heads):
            arrived(rest.at[t, s], r_rest.at[t, s])
    for s in range(heads):
        arrived(lrs.at[s], r_lr.at[s])
    tokens = heads * tb
    w1, w3, w2 = w0buf[0], w0buf[1], w0buf[2]
    first = (j == 0).astype(F32)

    def put(m, value):
        value = value + adj[m] * first
        tot[m * k:(m + 1) * k] = value.reshape(k, grain, dh)

    x, g = rest[2].reshape(tokens, dh), rest[3].reshape(tokens, dh)
    d_gate, d_up, hidden = query_terms(x, g, w1, w3, w2)
    put(0, two(tn, x, d_gate))
    put(1, two(tn, x, d_up))
    put(2, two(tn, hidden, g))
    send_back(0, two(nt, d_gate, w1) + two(nt, d_up, w3), dq_ref.at[0, :, cols(h)])

    keys, vals = rest[0].reshape(tokens, dh), rest[1].reshape(tokens, dh)
    base = base_ref[h]
    eta = jnp.concatenate(
        [jnp.broadcast_to(lrs[s][0:1], (tb, tb)).T[:, 0:1] for s in range(heads)], axis=0) * base
    a1, a3, a2 = split(adj[0]), split(adj[1]), split(adj[2])
    gate, up = nn(keys, w1), nn(keys, w3)
    d_hidden = eta * nt(vals, w2)
    proj1, proj3 = two(nn, keys, a1), two(nn, keys, a3)
    back = eta * two(nt, vals, a2)
    logistic, activated, slope = gate_terms(gate)
    curve = logistic * (1.0 - logistic) * (2.0 + gate * (1.0 - 2.0 * logistic))
    us = up * slope
    mixed = proj1 * us + proj3 * activated
    bar_gate = split(d_hidden * (proj1 * up * curve + proj3 * slope) + back * us)
    bar_up = split(d_hidden * proj1 * slope + back * activated)

    def more(m, value):
        tot[m * k:(m + 1) * k] += value.reshape(k, grain, dh)

    more(0, two(tn, keys, bar_gate))
    more(1, two(tn, keys, bar_up))
    more(2, two(tn, split(eta * mixed), vals))

    half = 3 * k // 2
    halves = []
    for i in range(half):
        c = pltpu.make_async_remote_copy(
            src_ref=tot.at[2 * i + 1 - core], dst_ref=sib.at[i], send_sem=s_half.at[i],
            recv_sem=r_half.at[i], device_id={"ctx": other}, device_id_type=MESH)
        c.start()
        halves.append(c)

    d_scaled = two(nn, split(mixed), w2) + two(nn, split(activated * up), a2)
    send_back(3, eta * d_scaled, dv_ref.at[:, cols(h)])
    rate = jnp.sum(vals.astype(F32) * d_scaled, axis=1, keepdims=True)
    acc = jnp.zeros((8, tb), F32)
    for s in range(heads):
        row = jnp.broadcast_to(rate[s * tb:(s + 1) * tb], (tb, tb)).T[0:8]
        rows[s] = row * base
        acc = acc + row * lrs[s]
    tile[...] = acc
    for step in range(heads):
        s = lax.rem(h + step, heads)
        go(Copy(me, s * group + j, rows.at[s], rate_ref.at[h], s_rate.at[step], r_rate.at[h]))
    for step in range(n):
        go(Copy(me, lax.rem(me + step, n), tile, part_ref.at[me], s_tile.at[step], r_tile.at[me]))

    key_grad = two(nt, bar_gate, w1) + two(nt, bar_up, w3)
    key_grad = key_grad + two(nt, split(d_hidden * us), a1)
    key_grad = key_grad + two(nt, split(d_hidden * activated), a3)
    send_back(2, key_grad, dk_ref.at[:, cols(h)])

    for i in range(half):
        halves[i].wait_recv()
        slot = 2 * i + core
        sib[i] = sib[i] + tot[slot]
        p = ((slot // k) * heads + h) * k + lax.rem(slot, k)
        go(Copy(me, p // own, sib.at[i], fbuf.at[lax.rem(p, own), chip], s_fin.at[i],
                r_fin.at[lax.rem(p, own), chip]))

    for pp in range(own):
        for c in range(chips):
            arrived(fbuf.at[pp, c], r_fin.at[pp, c])
        total = fbuf[pp, 0]
        for c in range(1, chips):
            total = total + fbuf[pp, c]
        fast_ref[pp] = total

    for s in range(heads):
        arrived(dq_ref.at[0, :, cols(s)], r_out.at[0, s])
        arrived(dq_ref.at[1, :, cols(s)], r_out.at[1, s])
        arrived(dk_ref.at[:, cols(s)], r_out.at[2, s])
        arrived(dv_ref.at[:, cols(s)], r_out.at[3, s])
        arrived(rate_ref.at[s], r_rate.at[s])
    for i in range(n):
        arrived(part_ref.at[i], r_tile.at[i])
    for c in sends:
        c.wait_send()
    for c in fwd + halves:
        c.wait_send()
    for d in range(1, chips):
        cc = lax.rem(chip + d, chips)
        for s in range(heads):
            pltpu.make_async_remote_copy(
                src_ref=line.at[cc * 2 + core, s], dst_ref=line.at[cc * 2 + core, s],
                send_sem=s_sib.at[cc, s], recv_sem=r_sib.at[cc, s],
                device_id={"ctx": other}, device_id_type=MESH).wait_send()
    for m in range(3):
        for r in range(k):
            slot = m * k + r
            owner = ((m * heads + h) * k + r) // own

            @pl.when(lax.rem(owner, 2) == core)
            def _():
                pltpu.make_async_remote_copy(
                    src_ref=w1buf.at[slot], dst_ref=w1buf.at[slot], send_sem=s_wf.at[slot],
                    recv_sem=r_w.at[slot], device_id={"ctx": other},
                    device_id_type=MESH).wait_send()


def gcd(a, b):
    while b:
        a, b = b, a % b
    return a


def local(n, queries, keys, values, lr_tok, lr_base, fast_init, fast_saved, dout):
    heads, dh = lr_base.shape[0], fast_init.shape[1]
    share, tb = fast_saved.shape[0], keys.shape[0]
    grain = gcd(share, dh)
    pad = -grain % 16
    k, own = dh // grain, share // grain
    group = n // heads
    chips = group // 2
    slots = 3 * k
    saved = jnp.pad(fast_saved.reshape(own, grain, dh), ((0, 0), (0, pad), (0, 0)))
    lr_rows = jnp.broadcast_to(lr_tok.T[:, None, :], (heads, 8, tb))
    dma = pltpu.SemaphoreType.DMA
    vmem = pl.BlockSpec(memory_space=pltpu.VMEM)
    anyw = pl.BlockSpec(memory_space=pl.ANY)
    width = heads * dh
    outs = pl.pallas_call(
        functools.partial(body, (n, heads, group, chips, tb, dh, grain, k, own)),
        out_shape=(
            jax.ShapeDtypeStruct((2, tb, width), BF),
            jax.ShapeDtypeStruct((tb, width), BF),
            jax.ShapeDtypeStruct((tb, width), BF),
            jax.ShapeDtypeStruct((heads, 8, tb), F32),
            jax.ShapeDtypeStruct((n, 8, tb), F32),
            jax.ShapeDtypeStruct((own, grain, dh), F32),
        ),
        in_specs=[anyw] * 4 + [vmem, pl.BlockSpec(memory_space=pltpu.SMEM), anyw, anyw],
        out_specs=tuple([vmem] * 6),
        scratch_shapes=[
            pltpu.VMEM((group, heads, 2, tb, dh), BF),
            pltpu.VMEM((4, heads, tb, dh), BF),
            pltpu.VMEM((heads, 8, tb), F32),
            pltpu.VMEM((slots, grain + pad, dh), BF),
            pltpu.VMEM((3, dh, dh), BF),
            pltpu.VMEM((3, dh, dh), F32),
            pltpu.VMEM((slots, grain, dh), F32),
            pltpu.VMEM((slots // 2, grain, dh), F32),
            pltpu.VMEM((own, chips, grain, dh), F32),
            pltpu.VMEM((4, heads, tb, dh), BF),
            pltpu.VMEM((heads, 8, tb), F32),
            pltpu.VMEM((8, tb), F32),
            dma((heads, 2)), dma((heads, 2)),
            dma((chips, heads)), dma((chips, heads)),
            dma((chips, heads)), dma((chips, heads)),
            dma((4, heads)), dma((4, heads)),
            dma((heads,)), dma((heads,)),
            dma((own, chips)), dma((slots,)), dma((slots,)),
            dma((3,)),
            dma((4, heads)), dma((4, heads)),
            dma((heads,)), dma((heads,)),
            dma((n,)), dma((n,)),
            dma((slots // 2,)), dma((slots // 2,)),
            dma((slots // 2,)), dma((own, chips)),
        ],
        compiler_params=pltpu.CompilerParams(
            collective_id=0, has_side_effects=True, vmem_limit_bytes=60 * 2**20),
    )(queries, dout, keys, values, lr_rows, lr_base, fast_init, saved)
    d_queries, d_keys, d_values, rate, part, fast = outs
    d_lr_tok = rate[:, 0, :].T
    base_grad = jnp.sum(part[:, 0, :].reshape(heads, -1), axis=1)
    return (d_queries, d_keys, d_values, d_lr_tok, base_grad, fast.reshape(share, dh))


def solution(mesh):
    both = ("grp", "ctx")
    rows = P(both, None)
    spans = P(None, both, None)
    in_specs = (spans, rows, rows, rows, P(), P(), rows, spans)
    out_specs = (spans, rows, rows, rows, P("grp"), rows)
    return jax.shard_map(
        functools.partial(local, mesh.shape["ctx"]), mesh=mesh, in_specs=in_specs,
        out_specs=out_specs, check_vma=False)
```
